32 devices in a mesh: gx: 2 (over x), gy: 4 (over y, core), ha: 4 (over z).
Axes of the slice: x: 2, y: 2, z: 4, core: 2. Of those that a mesh axis runs over, the one named last changes fastest.
Arguments:
- tokens: bfloat16 [16, 64, 16, 384], P('gx', 'gy'), may hold values from -30 to 30
- input_weight: bfloat16 [384, 768], P(None, 'ha'), may hold values from -1 to 1
- output_weight: bfloat16 [256, 384], P('ha'), may hold values from -0.375 to 0.375
- tissue_bits: int32 [16, 64], P('gx', 'gy'), may hold values from 0 to 65535
- cotangent: bfloat16 [16, 64, 16, 384], P('gx', 'gy'), may hold values from -6 to 6
Outputs:
- token_gradient: bfloat16 [16, 64, 16, 384], P('gx', 'gy', None, 'ha')
- input_gradient: float32 [384, 768], P(None, 'ha')
- output_gradient: float32 [256, 384], P('ha')
The draws below stay inside these ranges and needn't reach their ends.
All inputs are finite; a program needn't handle non-finite values.
Results may differ from the reference program's by a relative error of at most 0.018.
The reference program's roundings to bfloat16 on the way count: a program that leaves them out, or rounds other values in their place, can miss the bound.
Values may be sent and summed in bfloat16 or wider, within the bound.
A program may use at most 128 MiB of HBM per device.

```python
import jax
import jax.numpy as jnp
from jax import lax

D = 384
HEADS = 4
HD = 64
REACH = 3
DEPTH = 16
NX = 16
NY = 64
TOKENS = 16384


def draw_tokens(key, part):
    streams = jax.random.split(key, 1)
    base = jax.random.truncated_normal(streams[0], -4.0, 4.0, (NX, NY, DEPTH, D), jnp.float32)
    values = base
    return values.astype(jnp.bfloat16)


def draw_input_weight(key, part):
    base = jax.random.truncated_normal(key, -4.0, 4.0, (D, HEADS, 3, HD), jnp.float32) * D ** (-0.5)
    return base.reshape(D, HEADS * 3 * HD).astype(jnp.bfloat16)


def touch_ends(values, own_key, least, largest):
    place = [jax.random.randint(jax.random.fold_in(own_key, axis), (), 0, length) for axis, length in enumerate(values.shape)]
    longest = values.shape.index(max(values.shape))
    next_to = place[:longest] + [(place[longest] + 1) % values.shape[longest]] + place[longest + 1:]
    return values.at[tuple(place)].set(least).at[tuple(next_to)].set(largest)


def block_levels(own_key, dims, cuts, smallest, top_value):
    def one(axis_at, shards_of):
        draws = jax.random.uniform(jax.random.fold_in(jax.random.fold_in(own_key, 6), axis_at), (shards_of,), jnp.float32, smallest / len(cuts), top_value / len(cuts))
        return jnp.repeat(jnp.exp(draws), dims[axis_at] // shards_of).reshape((-1,) + (1,) * (len(dims) - axis_at - 1))

    loudness = one(*cuts[0])
    for cut in cuts[1:]:
        loudness = loudness * one(*cut)
    return loudness


def normal_values(own_key, extent, width, limit, cuts=(), kind=jnp.bfloat16):
    values = width * jax.random.normal(own_key, extent, jnp.float32)
    if cuts:
        values = values * block_levels(own_key, extent, cuts, -0.22, 0.18)
    return jnp.clip(values, -limit, limit).astype(kind)


def setup_inputs(seed: int = 0) -> dict:
    key_of = jax.random.split(jax.random.key(seed), 6)
    tokens = draw_tokens(jax.random.fold_in(key_of[5], 71), 0)
    input_weight = draw_input_weight(jax.random.fold_in(key_of[5], 71), 0)
    output_weight = normal_values(key_of[2], (HEADS * HD, D), (HEADS * HD) ** -0.5, 0.375, ((0, 4),))
    tissue_bits = touch_ends(jax.random.randint(key_of[3], (NX, NY), 0, 2 ** DEPTH), jax.random.fold_in(key_of[3], 1), 0, (2 ** DEPTH) - 1).astype(jnp.int32)
    cotangent = normal_values(key_of[4], (NX, NY, DEPTH, D), 1.0, 6.0, ((0, 2), (1, 4)))
    return dict(tokens=tokens, input_weight=input_weight, output_weight=output_weight, tissue_bits=tissue_bits, cotangent=cotangent)


def attend_head(entry, valid_padded):
    queries, keys, values, upstream = entry
    score_scale = HD ** -0.5
    window = 2 * REACH + 1
    pads = ((REACH, REACH), (REACH, REACH), (REACH, REACH), (0, 0))
    keys_padded = jnp.pad(keys, pads)
    values_padded = jnp.pad(values, pads)
    offset_index = jnp.arange(window ** 3, dtype=jnp.int32)
    offsets = jnp.stack([offset_index // (window * window), (offset_index // window) % window, offset_index % window], axis=1).astype(jnp.int32)
    centre = REACH * window * window + REACH * window + REACH
    query_float = queries.astype(jnp.float32)
    upstream_float = upstream.astype(jnp.float32)
    anchor = jnp.zeros((), jnp.int32)

    def shifted(array, offset):
        return lax.dynamic_slice(array, (offset[0], offset[1], offset[2], anchor), (NX, NY, DEPTH, HD))

    def score_at(pair):
        offset, position = pair
        keys_here = shifted(keys_padded, offset).astype(jnp.float32)
        scores = jnp.sum(query_float * keys_here, axis=-1) * score_scale
        live = lax.dynamic_slice(valid_padded, (offset[0], offset[1], offset[2]), (NX, NY, DEPTH)) > 0
        return jnp.where(live | (position == centre), scores, -jnp.inf)

    scores = lax.map(score_at, (offsets, offset_index))
    row_max = jnp.max(scores, axis=0)
    raised = jnp.exp(scores - row_max)
    totals = jnp.sum(raised, axis=0)
    weights = (raised / totals).astype(jnp.bfloat16)

    def accumulate(running, pair):
        offset, weight = pair
        values_here = shifted(values_padded, offset).astype(jnp.float32)
        return running + weight.astype(jnp.float32)[..., None] * values_here, None

    output, _ = lax.scan(accumulate, jnp.zeros((NX, NY, DEPTH, HD), jnp.float32), (offsets, weights))
    attended = output.astype(jnp.bfloat16)
    row_inner = jnp.sum(upstream_float * output, axis=-1)
    padded_shape = (NX + 2 * REACH, NY + 2 * REACH, DEPTH + 2 * REACH, HD)

    def backward(carry, pair):
        query_sum, key_sum, value_sum = carry
        offset, weight = pair
        keys_here = shifted(keys_padded, offset).astype(jnp.float32)
        values_here = shifted(values_padded, offset).astype(jnp.float32)
        weight_here = weight.astype(jnp.float32)
        weight_gradient = jnp.sum(upstream_float * values_here, axis=-1)
        score_gradient = lax.optimization_barrier((weight_here * (weight_gradient - row_inner) * score_scale).astype(jnp.bfloat16)).astype(jnp.float32)
        query_sum = query_sum + score_gradient[..., None] * keys_here
        first = (offset[0], offset[1], offset[2], anchor)
        key_sum = lax.dynamic_update_slice(key_sum, shifted(key_sum, offset) + score_gradient[..., None] * query_float, first)
        value_sum = lax.dynamic_update_slice(value_sum, shifted(value_sum, offset) + weight_here[..., None] * upstream_float, first)
        return (query_sum, key_sum, value_sum), None

    start = (jnp.zeros((NX, NY, DEPTH, HD), jnp.float32), jnp.zeros(padded_shape, jnp.float32), jnp.zeros(padded_shape, jnp.float32))
    (query_sum, key_sum, value_sum), _ = lax.scan(backward, start, (offsets, weights))
    key_inner = key_sum[REACH:REACH + NX, REACH:REACH + NY, REACH:REACH + DEPTH]
    value_inner = value_sum[REACH:REACH + NX, REACH:REACH + NY, REACH:REACH + DEPTH]
    return attended, query_sum, key_inner, value_inner


def heads_leading(array):
    return jnp.moveaxis(array, 3, 0)


def reference(tokens, input_weight, output_weight, tissue_bits, cotangent):
    flat_tokens = tokens.reshape(TOKENS, D)
    flat_cotangent = cotangent.reshape(TOKENS, D)
    projected = jnp.dot(flat_tokens, input_weight, preferred_element_type=jnp.float32).astype(jnp.bfloat16)
    projected = projected.reshape(NX, NY, DEPTH, HEADS, 3, HD)
    upstream = jnp.dot(flat_cotangent, output_weight.T, preferred_element_type=jnp.float32).astype(jnp.bfloat16)
    upstream = upstream.reshape(NX, NY, DEPTH, HEADS, HD)
    bit_values = 2 ** jnp.arange(DEPTH, dtype=jnp.int32)
    key_valid = ((tissue_bits[:, :, None] // bit_values) % 2).astype(jnp.float32)
    valid_padded = jnp.pad(key_valid, REACH)

    def one_head(entry):
        return attend_head(entry, valid_padded)

    entries = (heads_leading(projected[:, :, :, :, 0, :]), heads_leading(projected[:, :, :, :, 1, :]), heads_leading(projected[:, :, :, :, 2, :]), heads_leading(upstream))
    attended, query_grads, key_grads, value_grads = lax.map(one_head, entries)
    stacked = jnp.stack([query_grads, key_grads, value_grads], axis=4)
    dprojected = jnp.moveaxis(stacked, 0, 3).astype(jnp.bfloat16).reshape(TOKENS, HEADS * 3 * HD)
    attended_flat = jnp.moveaxis(attended, 0, 3).reshape(TOKENS, HEADS * HD)
    token_gradient = jnp.dot(dprojected, input_weight.T, preferred_element_type=jnp.float32).astype(jnp.bfloat16)
    token_gradient = token_gradient.reshape(NX, NY, DEPTH, D)
    normaliser = TOKENS ** -0.5
    input_gradient = jnp.dot(flat_tokens.T, dprojected, preferred_element_type=jnp.float32) * normaliser
    output_gradient = jnp.dot(attended_flat.T, flat_cotangent, preferred_element_type=jnp.float32) * normaliser
    return token_gradient, input_gradient, output_gradient
```

```python
import functools

import jax
import jax.numpy as jnp
import numpy as np
from jax import lax
from jax.experimental import pallas as pl
from jax.experimental.pallas import tpu as pltpu
from jax.sharding import PartitionSpec as P

HD = 64
REACH = 3
VMEM = pl.BlockSpec(memory_space=pltpu.VMEM)
SMEM = pl.BlockSpec(memory_space=pltpu.SMEM)


def dot(a, b, ca, cb):
    return lax.dot_general(a, b, (((ca,), (cb,)), ((), ())), preferred_element_type=jnp.float32)


def shift(array, axis, up):
    count = lax.axis_size(axis)
    pairs = [(i, i + 1) for i in range(count - 1)]
    if not up:
        pairs = [(b, a) for a, b in pairs]
    return lax.ppermute(array, axis, pairs)


def tile_of(extent):
    return 4 if extent % 4 == 0 else extent


def mask_table(bx, by, depth):
    kx, ky = bx + 2 * REACH, by + 2 * REACH
    kg = np.stack(np.meshgrid(np.arange(kx) - REACH, np.arange(ky) - REACH, np.arange(depth), indexing="ij"), -1)
    qg = np.stack(np.meshgrid(np.arange(bx), np.arange(by), np.arange(depth), indexing="ij"), -1)
    far = np.abs(kg.reshape(-1, 1, 3) - qg.reshape(1, -1, 3)).max(-1)
    return ((far <= REACH).astype(np.float32) + (far == 0)).astype(np.float32)


def attend_kernel(
    depth, bx, by, tok, cot, wq, wo, kv, xlo, xhi, ylo, yhi, bits, table, dq_ref, acc, wg, kvp, gate
):
    nx, ny = tok.shape[0], tok.shape[1] // depth
    rim = REACH * depth
    rows = ny * depth
    scale = HD ** (-0.5)
    kvp[REACH : REACH + nx, rim : rim + rows] = kv[...]
    kvp[:REACH, rim : rim + rows] = xlo[...]
    kvp[REACH + nx :, rim : rim + rows] = xhi[...]
    kvp[:, :rim] = ylo[...]
    kvp[:, rim + rows :] = yhi[...]
    acc[...] = jnp.zeros_like(acc)
    wg[...] = jnp.zeros_like(wg)
    z = lax.broadcasted_iota(jnp.int32, (depth, 128), 0)

    def fill(x, carry):
        for y in range(ny + 2 * REACH):
            live = jnp.right_shift(jnp.full((depth, 128), bits[x, y], jnp.int32), z) & 1
            gate[x, y * depth : (y + 1) * depth, :] = 1.0 - live.astype(jnp.float32)
        return carry

    lax.fori_loop(0, nx + 2 * REACH, fill, 0)
    kx, kr = bx + 2 * REACH, (by + 2 * REACH) * depth
    qr = by * depth
    nq, nk = bx * qr, kx * kr
    across = ny // by

    def body(i, carry):
        x0 = (i // across) * bx
        r0 = pl.multiple_of((i % across) * qr, qr)
        mine = (pl.ds(x0, bx), pl.ds(r0, qr))
        wide = (pl.ds(x0, kx), pl.ds(r0, kr))
        tb = tok[mine].reshape(nq, -1)
        cb = cot[mine].reshape(nq, -1)
        q = (dot(tb, wq[...], 1, 0).astype(jnp.bfloat16).astype(jnp.float32) * scale).astype(jnp.bfloat16)
        u = dot(cb, wo[...], 1, 1).astype(jnp.bfloat16)
        keys = kvp[wide].reshape(nk, 2 * HD)
        g1 = gate[wide].reshape(nk, 128)
        g1 = jnp.concatenate([g1] * (nq // 128), axis=1)
        s = jnp.where(table[...] > g1, dot(keys, q, 1, 1), -1e30)
        e = jnp.exp(s - jnp.max(s, axis=0, keepdims=True))
        p = (e * (1.0 / jnp.sum(e, axis=0, keepdims=True))).astype(jnp.bfloat16)
        o = dot(keys, p, 0, 0)
        r = jnp.sum(u.astype(jnp.float32).T * o, axis=0, keepdims=True)
        g = dot(keys, u, 1, 1)
        ds = (p.astype(jnp.float32) * (g - r)).astype(jnp.bfloat16)
        dq = dot(keys, ds, 0, 0) * scale
        dkv = dot(ds, q, 1, 0) + dot(p, u, 1, 0)
        acc[wide] += dkv.reshape(kx, kr, 2 * HD)
        wg[:HD] += dot(dq[:HD].astype(jnp.bfloat16), tb, 1, 0)
        wg[HD:] += dot(o[HD:].astype(jnp.bfloat16), cb, 1, 0)
        dq_ref[mine] = dq.T.astype(jnp.bfloat16).reshape(bx, qr, 2 * HD)
        return carry

    lax.fori_loop(0, (nx // bx) * across, body, 0)


def tail_kernel(rim, tok, dq, acc, xlo, xhi, ylo, yhi, wq, wkv, wg, part, grads, cen):
    nx, rows = tok.shape[0], tok.shape[1]
    cen[...] = acc[REACH : REACH + nx, rim : rim + rows]
    cen[:REACH] += xlo[:, rim : rim + rows].astype(jnp.float32)
    cen[nx - REACH :] += xhi[:, rim : rim + rows].astype(jnp.float32)
    cen[:, :rim] += ylo[...].astype(jnp.float32)
    cen[:, rows - rim :] += yhi[...].astype(jnp.float32)
    total = jnp.zeros((2 * HD, tok.shape[2]), jnp.float32)
    for x in range(nx):
        dkv = cen[x].astype(jnp.bfloat16)
        part[x] = (dot(dkv, wkv[...], 1, 1) + dot(dq[x], wq[...], 1, 1)).astype(jnp.bfloat16)
        total += dot(dkv, tok[x], 0, 0)
    grads[: 2 * HD] = wg[...].astype(jnp.bfloat16)
    grads[2 * HD :] = total.astype(jnp.bfloat16)


def window_bits(tissue_bits):
    nx, ny = tissue_bits.shape
    whole = lax.all_gather(tissue_bits, ("gx", "gy"))
    cx, cy = lax.axis_size("gx"), lax.axis_size("gy")
    whole = whole.reshape(cx, cy, nx, ny).transpose(0, 2, 1, 3).reshape(cx * nx, cy * ny)
    whole = jnp.pad(whole, REACH)
    start = (lax.axis_index("gx") * nx, lax.axis_index("gy") * ny)
    return lax.dynamic_slice(whole, start, (nx + 2 * REACH, ny + 2 * REACH))


def shards(tokens, input_weight, output_weight, tissue_bits, cotangent):
    nx, ny, depth, width = tokens.shape
    rows, rim = ny * depth, REACH * depth
    tok = tokens.reshape(nx, rows, width)
    cot = cotangent.reshape(nx, rows, width)
    wq = jnp.pad(input_weight[:, :HD], ((0, 0), (0, HD)))
    wkv = input_weight[:, HD:]
    wo = jnp.pad(output_weight, ((HD, 0), (0, 0)))
    bits = window_bits(tissue_bits)
    kv = (
        jnp.dot(tok.reshape(nx * rows, width), wkv, preferred_element_type=jnp.float32)
        .astype(jnp.bfloat16)
        .reshape(nx, rows, 2 * HD)
    )
    xlo = shift(kv[nx - REACH :], "gx", True)
    xhi = shift(kv[:REACH], "gx", False)
    top = jnp.concatenate([xlo[:, rows - rim :], kv[:, rows - rim :], xhi[:, rows - rim :]], axis=0)
    bottom = jnp.concatenate([xlo[:, :rim], kv[:, :rim], xhi[:, :rim]], axis=0)
    ylo = shift(top, "gy", True)
    yhi = shift(bottom, "gy", False)
    bx, by = tile_of(nx), tile_of(ny)
    table = jnp.asarray(mask_table(bx, by, depth))
    px, pr = nx + 2 * REACH, rows + 2 * rim
    dq, acc, wg = pl.pallas_call(
        functools.partial(attend_kernel, depth, bx, by),
        out_shape=(
            jax.ShapeDtypeStruct((nx, rows, 2 * HD), jnp.bfloat16),
            jax.ShapeDtypeStruct((px, pr, 2 * HD), jnp.float32),
            jax.ShapeDtypeStruct((2 * HD, width), jnp.float32),
        ),
        in_specs=[VMEM] * 9 + [SMEM, VMEM],
        out_specs=(VMEM,) * 3,
        scratch_shapes=[
            pltpu.VMEM((px, pr, 2 * HD), jnp.bfloat16),
            pltpu.VMEM((px, pr, 128), jnp.float32),
        ],
        compiler_params=pltpu.CompilerParams(vmem_limit_bytes=48 * 1024 * 1024),
        name="attend",
    )(tok, cot, wq, wo, kv, xlo, xhi, ylo, yhi, bits, table)

    dxlo = shift(acc[REACH + nx :].astype(jnp.bfloat16), "gx", True)
    dxhi = shift(acc[:REACH].astype(jnp.bfloat16), "gx", False)

    def edge(lo, hi):
        mine = acc[REACH : REACH + nx, lo:hi]
        below = jnp.pad(dxlo[:, lo:hi].astype(jnp.float32), ((0, nx - REACH), (0, 0), (0, 0)))
        above = jnp.pad(dxhi[:, lo:hi].astype(jnp.float32), ((nx - REACH, 0), (0, 0), (0, 0)))
        return (mine + below + above).astype(jnp.bfloat16)

    dylo = shift(edge(rim + rows, pr), "gy", True)
    dyhi = shift(edge(0, rim), "gy", False)
    part, grads = pl.pallas_call(
        functools.partial(tail_kernel, rim),
        out_shape=(
            jax.ShapeDtypeStruct((nx, rows, width), jnp.bfloat16),
            jax.ShapeDtypeStruct((4 * HD, width), jnp.bfloat16),
        ),
        in_specs=[VMEM] * 10,
        out_specs=(VMEM,) * 2,
        scratch_shapes=[pltpu.VMEM((nx, rows, 2 * HD), jnp.float32)],
        compiler_params=pltpu.CompilerParams(vmem_limit_bytes=48 * 1024 * 1024),
        name="tail",
    )(tok, dq, acc, dxlo, dxhi, dylo, dyhi, wq, wkv, wg)
    token_gradient = lax.psum_scatter(
        part.reshape(nx * rows, width), "ha", scatter_dimension=1, tiled=True
    ).reshape(nx, ny, depth, -1)
    count = nx * rows * lax.axis_size("gx") * lax.axis_size("gy")
    summed = lax.psum(grads, ("gx", "gy")).astype(jnp.float32) * count ** (-0.5)
    turned = jnp.concatenate([summed[:HD], summed[2 * HD :]], axis=0).T
    return token_gradient, turned, summed[HD : 2 * HD]


def solution(mesh):
    placed = (
        P("gx", "gy", None, None),
        P(None, "ha"),
        P("ha", None),
        P("gx", "gy"),
        P("gx", "gy", None, None),
    )
    return jax.shard_map(
        shards,
        mesh=mesh,
        in_specs=placed,
        out_specs=(P("gx", "gy", None, "ha"), P(None, "ha"), P("ha", None)),
        check_vma=False,
    )
```

```python
import functools

import jax
import jax.numpy as jnp
import numpy as np
from jax import lax
from jax.experimental import pallas as pl
from jax.experimental.pallas import tpu as pltpu
from jax.sharding import PartitionSpec as P

HD = 64
REACH = 3
VMEM = pl.BlockSpec(memory_space=pltpu.VMEM)
SMEM = pl.BlockSpec(memory_space=pltpu.SMEM)
MESH = pl.DeviceIdType.MESH


def dot(a, b, ca, cb):
    return lax.dot_general(a, b, (((ca,), (cb,)), ((), ())), preferred_element_type=jnp.float32)


def tile_of(extent):
    return 4 if extent % 4 == 0 else extent


def mask_table(bx, by, depth):
    kx, ky = bx + 2 * REACH, by + 2 * REACH
    kg = np.stack(np.meshgrid(np.arange(kx) - REACH, np.arange(ky) - REACH, np.arange(depth), indexing="ij"), -1)
    qg = np.stack(np.meshgrid(np.arange(bx), np.arange(by), np.arange(depth), indexing="ij"), -1)
    far = np.abs(kg.reshape(-1, 1, 3) - qg.reshape(1, -1, 3)).max(-1)
    return ((far <= REACH).astype(np.float32) + (far == 0)).astype(np.float32)


def send(src, dst, send_sem, recv_sem, where):
    return pltpu.make_async_remote_copy(
        src_ref=src, dst_ref=dst, send_sem=send_sem, recv_sem=recv_sem, device_id=where, device_id_type=MESH
    )


def swap(axis, count, to_low, to_high):
    me = lax.axis_index(axis)
    has_low, has_high = me > 0, me < count - 1

    @pl.when(has_low)
    def _():
        to_low.start()

    @pl.when(has_high)
    def _():
        to_high.start()

    @pl.when(has_low)
    def _():
        to_low.wait_send()
        to_high.wait_recv()

    @pl.when(has_high)
    def _():
        to_high.wait_send()
        to_low.wait_recv()


def kernel(
    sizes, depth, bx, by, tok, cot, wq, wkv, wo, bits, table,
    token_out, input_out, output_out,
    kvg, acc, wg, dq_all, cen, dkv_all, sx, rx, sy, ry, psend, precv, own, gsrc, grecv, gsum,
    sem_h, sem_hr, sem_p, sem_pr, sem_g, sem_gr, sem_b, sem_br,
):
    cx, cy, ch = sizes
    nx, rows = tok.shape[0], tok.shape[1]
    ny, width = rows // depth, tok.shape[2]
    rim = REACH * depth
    scale = HD ** (-0.5)
    ix, iy, ih = lax.axis_index("gx"), lax.axis_index("gy"), lax.axis_index("ha")
    n = cx * cy
    flat = ix * cy + iy

    def peer(k):
        t = lax.rem(flat + k, n)
        return t, {"gx": t // cy, "gy": lax.rem(t, cy)}

    barrier = pltpu.get_barrier_semaphore()
    for k in range(1, n):
        pl.semaphore_signal(barrier, inc=1, device_id=peer(k)[1], device_id_type=MESH)
    for k in range(1, ch):
        pl.semaphore_signal(barrier, inc=1, device_id={"ha": lax.rem(ih + k, ch)}, device_id_type=MESH)

    z = lax.broadcasted_iota(jnp.int32, (depth, 128), 0)

    def fill(x, carry):
        kvg[REACH + x, rim : rim + rows, : 2 * HD] = dot(tok[x], wkv[...], 1, 0).astype(jnp.bfloat16)
        for y in range(ny):
            live = jnp.right_shift(jnp.full((depth, 128), bits[x, y], jnp.int32), z) & 1
            kvg[REACH + x, rim + y * depth : rim + (y + 1) * depth, 2 * HD :] = (
                1.0 - live.astype(jnp.float32)
            ).astype(jnp.bfloat16)
        return carry

    lax.fori_loop(0, nx, fill, 0)

    def blank(where_x, where_r):
        shape = kvg.at[where_x, where_r, : 2 * HD].shape
        kvg[where_x, where_r, : 2 * HD] = jnp.zeros(shape, jnp.bfloat16)
        kvg[where_x, where_r, 2 * HD :] = jnp.ones(shape, jnp.bfloat16)

    xs_low, xs_high = slice(0, REACH), slice(REACH + nx, nx + 2 * REACH)
    rs_low, rs_mid, rs_high = slice(0, rim), slice(rim, rim + rows), slice(rim + rows, rows + 2 * rim)
    pl.when(ix == 0)(lambda: blank(xs_low, rs_mid))
    pl.when(ix == cx - 1)(lambda: blank(xs_high, rs_mid))
    pl.when(iy == 0)(lambda: blank(slice(None), rs_low))
    pl.when(iy == cy - 1)(lambda: blank(slice(None), rs_high))

    pl.semaphore_wait(barrier, n - 1 + ch - 1)
    swap(
        "gx", cx,
        send(kvg.at[REACH : 2 * REACH, rs_mid], kvg.at[xs_high, rs_mid], sem_h.at[0], sem_hr.at[0], {"gx": ix - 1}),
        send(kvg.at[nx : nx + REACH, rs_mid], kvg.at[xs_low, rs_mid], sem_h.at[1], sem_hr.at[1], {"gx": ix + 1}),
    )
    swap(
        "gy", cy,
        send(kvg.at[:, rim : 2 * rim], kvg.at[:, rs_high], sem_h.at[2], sem_hr.at[2], {"gy": iy - 1}),
        send(kvg.at[:, rows : rows + rim], kvg.at[:, rs_low], sem_h.at[3], sem_hr.at[3], {"gy": iy + 1}),
    )

    acc[...] = jnp.zeros_like(acc)
    wg[...] = jnp.zeros_like(wg)
    kx, kr = bx + 2 * REACH, (by + 2 * REACH) * depth
    qr = by * depth
    nq, nk = bx * qr, kx * kr
    across = ny // by

    def body(i, carry):
        x0 = (i // across) * bx
        r0 = pl.multiple_of(lax.rem(i, across) * qr, qr)
        mine = (pl.ds(x0, bx), pl.ds(r0, qr))
        wide = (pl.ds(x0, kx), pl.ds(r0, kr))
        tb = tok[mine].reshape(nq, -1)
        cb = cot[mine].reshape(nq, -1)
        q = (dot(tb, wq[...], 1, 0).astype(jnp.bfloat16).astype(jnp.float32) * scale).astype(jnp.bfloat16)
        u = dot(cb, wo[...], 1, 1).astype(jnp.bfloat16)
        keys = kvg[pl.ds(x0, kx), pl.ds(r0, kr), : 2 * HD].reshape(nk, 2 * HD)
        g1 = kvg[pl.ds(x0, kx), pl.ds(r0, kr), 2 * HD :].reshape(nk, 128).astype(jnp.float32)
        g1 = jnp.concatenate([g1] * (nq // 128), axis=1)
        s = jnp.where(table[...] > g1, dot(keys, q, 1, 1), -1e30)
        e = jnp.exp(s - jnp.max(s, axis=0, keepdims=True))
        p = (e * (1.0 / jnp.sum(e, axis=0, keepdims=True))).astype(jnp.bfloat16)
        o = dot(keys, p, 0, 0)
        r = jnp.sum(u.astype(jnp.float32).T * o, axis=0, keepdims=True)
        g = dot(keys, u, 1, 1)
        ds = (p.astype(jnp.float32) * (g - r)).astype(jnp.bfloat16)
        dq = dot(keys, ds, 0, 0) * scale
        dkv = dot(ds, q, 1, 0) + dot(p, u, 1, 0)
        acc[wide] += dkv.reshape(kx, kr, 2 * HD)
        wg[:HD] += dot(dq[:HD].astype(jnp.bfloat16), tb, 1, 0)
        wg[HD:] += dot(o[HD:].astype(jnp.bfloat16), cb, 1, 0)
        dq_all[mine] = dq.T.astype(jnp.bfloat16).reshape(bx, qr, 2 * HD)
        return carry

    lax.fori_loop(0, (nx // bx) * across, body, 0)

    sx[0] = acc[:REACH].astype(jnp.bfloat16)
    sx[1] = acc[REACH + nx :].astype(jnp.bfloat16)
    swap(
        "gx", cx,
        send(sx.at[0], rx.at[1], sem_h.at[4], sem_hr.at[4], {"gx": ix - 1}),
        send(sx.at[1], rx.at[0], sem_h.at[5], sem_hr.at[5], {"gx": ix + 1}),
    )
    cen[...] = acc[REACH : REACH + nx]

    @pl.when(ix > 0)
    def _():
        cen[:REACH] += rx[0].astype(jnp.float32)

    @pl.when(ix < cx - 1)
    def _():
        cen[nx - REACH :] += rx[1].astype(jnp.float32)

    sy[0] = cen[:, :rim].astype(jnp.bfloat16)
    sy[1] = cen[:, rim + rows :].astype(jnp.bfloat16)
    swap(
        "gy", cy,
        send(sy.at[0], ry.at[1], sem_h.at[6], sem_hr.at[6], {"gy": iy - 1}),
        send(sy.at[1], ry.at[0], sem_h.at[7], sem_hr.at[7], {"gy": iy + 1}),
    )

    @pl.when(iy > 0)
    def _():
        cen[:, rim : 2 * rim] += ry[0].astype(jnp.float32)

    @pl.when(iy < cy - 1)
    def _():
        cen[:, rows : rows + rim] += ry[1].astype(jnp.float32)

    dkv_all[...] = cen[:, rs_mid].astype(jnp.bfloat16)
    share = width // ch

    def product(j):
        cols = pl.ds(pl.multiple_of(j * share, 16), share)
        dkv = dkv_all[...].reshape(nx * rows, 2 * HD)
        dqs = dq_all[...].reshape(nx * rows, 2 * HD)
        return dot(wkv[cols, :], dkv, 1, 1) + dot(wq[cols, :], dqs, 1, 1)

    parts = []
    for k in range(1, ch):
        j = lax.rem(ih + k, ch)
        psend[k - 1] = product(j).astype(jnp.bfloat16)
        copy = send(psend.at[k - 1], precv.at[k - 1], sem_p.at[k - 1], sem_pr.at[k - 1], {"ha": j})
        copy.start()
        parts.append(copy)

    gsrc[: 2 * HD] = wg[...]
    gsrc[2 * HD :] = dot(
        dkv_all[...].reshape(nx * rows, 2 * HD), tok[...].reshape(nx * rows, width), 0, 0
    )
    piece = 4 * HD // n
    first = []
    for k in range(1, n):
        t, where = peer(k)
        src = gsrc.at[pl.ds(pl.multiple_of(t * piece, 8), piece)]
        copy = send(src, grecv.at[k - 1], sem_g.at[k - 1], sem_gr.at[k - 1], where)
        copy.start()
        first.append(copy)
    own[...] = product(ih)
    mine = pl.ds(pl.multiple_of(flat * piece, 8), piece)
    total = gsrc[mine]
    for k in range(1, n):
        first[k - 1].wait_recv()
        total += grecv[k - 1]
    gsum[mine] = total
    second = []
    for k in range(1, n):
        copy = send(gsum.at[mine], gsum.at[mine], sem_b.at[k - 1], sem_br.at[k - 1], peer(k)[1])
        copy.start()
        second.append(copy)
    for copy in first:
        copy.wait_send()
    for k in range(1, n):
        t = lax.rem(flat + n - k, n)
        other = gsum.at[pl.ds(pl.multiple_of(t * piece, 8), piece)]
        send(other, other, sem_b.at[k - 1], sem_br.at[k - 1], peer(k)[1]).wait_recv()
    for copy in second:
        copy.wait_send()
    norm = (n * nx * rows) ** (-0.5)
    everything = gsum[...] * norm
    output_out[...] = everything[HD : 2 * HD]
    input_out[...] = jnp.concatenate([everything[:HD], everything[2 * HD :]], axis=0).T
    for copy in parts:
        copy.wait()
    summed = own[...]
    for k in range(1, ch):
        summed += precv[k - 1].astype(jnp.float32)
    token_out[...] = summed.T.astype(jnp.bfloat16)


def shards(tokens, input_weight, output_weight, tissue_bits, cotangent):
    nx, ny, depth, width = tokens.shape
    rows, rim = ny * depth, REACH * depth
    sizes = tuple(lax.axis_size(a) for a in ("gx", "gy", "ha"))
    n, ch = sizes[0] * sizes[1], sizes[2]
    tok = tokens.reshape(nx, rows, width)
    cot = cotangent.reshape(nx, rows, width)
    wq = jnp.pad(input_weight[:, :HD], ((0, 0), (0, HD)))
    wkv = input_weight[:, HD:]
    wo = jnp.pad(output_weight, ((HD, 0), (0, 0)))
    bx, by = tile_of(nx), tile_of(ny)
    table = jnp.asarray(mask_table(bx, by, depth))
    px, pr = nx + 2 * REACH, rows + 2 * rim
    bf, f32, dma = jnp.bfloat16, jnp.float32, pltpu.SemaphoreType.DMA
    share = width // ch
    token_gradient, input_gradient, output_gradient = pl.pallas_call(
        functools.partial(kernel, sizes, depth, bx, by),
        out_shape=(
            jax.ShapeDtypeStruct((nx * rows, share), bf),
            jax.ShapeDtypeStruct((width, 3 * HD), f32),
            jax.ShapeDtypeStruct((HD, width), f32),
        ),
        in_specs=[VMEM] * 5 + [SMEM, VMEM],
        out_specs=(VMEM,) * 3,
        scratch_shapes=[
            pltpu.VMEM((px, pr, 4 * HD), bf),
            pltpu.VMEM((px, pr, 2 * HD), f32),
            pltpu.VMEM((2 * HD, width), f32),
            pltpu.VMEM((nx, rows, 2 * HD), bf),
            pltpu.VMEM((nx, pr, 2 * HD), f32),
            pltpu.VMEM((nx, rows, 2 * HD), bf),
            pltpu.VMEM((2, REACH, pr, 2 * HD), bf),
            pltpu.VMEM((2, REACH, pr, 2 * HD), bf),
            pltpu.VMEM((2, nx, rim, 2 * HD), bf),
            pltpu.VMEM((2, nx, rim, 2 * HD), bf),
            pltpu.VMEM((ch - 1, share, nx * rows), bf),
            pltpu.VMEM((ch - 1, share, nx * rows), bf),
            pltpu.VMEM((share, nx * rows), f32),
            pltpu.VMEM((4 * HD, width), f32),
            pltpu.VMEM((n - 1, 4 * HD // n, width), f32),
            pltpu.VMEM((4 * HD, width), f32),
            dma((8,)), dma((8,)),
            dma((ch - 1,)), dma((ch - 1,)),
            dma((n - 1,)), dma((n - 1,)),
            dma((n - 1,)), dma((n - 1,)),
        ],
        compiler_params=pltpu.CompilerParams(
            collective_id=0, has_side_effects=True, vmem_limit_bytes=56 * 1024 * 1024
        ),
        name="whole",
    )(tok, cot, wq, wkv, wo, tissue_bits, table)
    return token_gradient.reshape(nx, ny, depth, share), input_gradient, output_gradient


def solution(mesh):
    placed = (
        P("gx", "gy", None, None),
        P(None, "ha"),
        P("ha", None),
        P("gx", "gy"),
        P("gx", "gy", None, None),
    )
    return jax.shard_map(
        shards,
        mesh=mesh,
        in_specs=placed,
        out_specs=(P("gx", "gy", None, "ha"), P(None, "ha"), P("ha", None)),
        check_vma=False,
    )
```

```python
import functools

import jax
import jax.numpy as jnp
import numpy as np
from jax import lax
from jax.experimental import pallas as pl
from jax.experimental.pallas import tpu as pltpu
from jax.sharding import PartitionSpec as P

HD = 64
REACH = 3
VMEM = pl.BlockSpec(memory_space=pltpu.VMEM)
SMEM = pl.BlockSpec(memory_space=pltpu.SMEM)
MESH = pl.DeviceIdType.MESH


def dot(a, b, ca, cb):
    return lax.dot_general(a, b, (((ca,), (cb,)), ((), ())), preferred_element_type=jnp.float32)


def tile_of(extent):
    return 4 if extent % 4 == 0 else extent


def mask_table(bx, by, depth):
    kx, ky = bx + 2 * REACH, by + 2 * REACH
    kg = np.stack(np.meshgrid(np.arange(kx) - REACH, np.arange(ky) - REACH, np.arange(depth), indexing="ij"), -1)
    qg = np.stack(np.meshgrid(np.arange(bx), np.arange(by), np.arange(depth), indexing="ij"), -1)
    far = np.abs(kg.reshape(-1, 1, 3) - qg.reshape(1, -1, 3)).max(-1)
    return ((far <= REACH).astype(np.float32) + (far == 0)).astype(np.float32)


def send(src, dst, send_sem, recv_sem, where):
    return pltpu.make_async_remote_copy(
        src_ref=src, dst_ref=dst, send_sem=send_sem, recv_sem=recv_sem, device_id=where, device_id_type=MESH
    )


def swap(axis, count, to_low, to_high):
    me = lax.axis_index(axis)
    has_low, has_high = me > 0, me < count - 1

    @pl.when(has_low)
    def _():
        to_low.start()

    @pl.when(has_high)
    def _():
        to_high.start()

    @pl.when(has_low)
    def _():
        to_low.wait_send()
        to_high.wait_recv()

    @pl.when(has_high)
    def _():
        to_high.wait_send()
        to_low.wait_recv()


def kernel(
    sizes, depth, bx, by, tok, cot, weights, outer, bits, table,
    token_out, input_out, output_out,
    wq, wkv, wo, kvg, acc, wg, dq_all, cen, dkv_all, sx, rx, sy, ry, psend, precv, own, gsrc, grecv, gsum,
    sem_h, sem_hr, sem_p, sem_pr, sem_g, sem_gr, sem_b, sem_br,
):
    cx, cy, ch = sizes
    nx, rows = tok.shape[0], tok.shape[1]
    ny, width = rows // depth, tok.shape[2]
    rim = REACH * depth
    scale = HD ** (-0.5)
    ix, iy, ih = lax.axis_index("gx"), lax.axis_index("gy"), lax.axis_index("ha")
    n = cx * cy
    flat = ix * cy + iy

    def peer(k):
        t = lax.rem(flat + k, n)
        return t, {"gx": t // cy, "gy": lax.rem(t, cy)}

    barrier = pltpu.get_barrier_semaphore()
    for k in range(1, n):
        pl.semaphore_signal(barrier, inc=1, device_id=peer(k)[1], device_id_type=MESH)
    for k in range(1, ch):
        pl.semaphore_signal(barrier, inc=1, device_id={"ha": lax.rem(ih + k, ch)}, device_id_type=MESH)

    turned = weights[...].astype(jnp.float32)
    blank_rows = jnp.zeros((HD, width), jnp.float32)
    wq[...] = jnp.concatenate([turned[:HD], blank_rows], axis=0).T.astype(jnp.bfloat16)
    wkv[...] = turned[HD:].T.astype(jnp.bfloat16)
    wo[:HD] = blank_rows.astype(jnp.bfloat16)
    wo[HD:] = outer[...]
    z = lax.broadcasted_iota(jnp.int32, (depth, 128), 0)

    def fill(x, carry):
        kvg[REACH + x, rim : rim + rows, : 2 * HD] = dot(tok[x], wkv[...], 1, 0).astype(jnp.bfloat16)
        for y in range(ny):
            live = jnp.right_shift(jnp.full((depth, 128), bits[x, y], jnp.int32), z) & 1
            kvg[REACH + x, rim + y * depth : rim + (y + 1) * depth, 2 * HD :] = (
                1.0 - live.astype(jnp.float32)
            ).astype(jnp.bfloat16)
        return carry

    lax.fori_loop(0, nx, fill, 0)

    def blank(where_x, where_r):
        shape = kvg.at[where_x, where_r, : 2 * HD].shape
        kvg[where_x, where_r, : 2 * HD] = jnp.zeros(shape, jnp.bfloat16)
        kvg[where_x, where_r, 2 * HD :] = jnp.ones(shape, jnp.bfloat16)

    xs_low, xs_high = slice(0, REACH), slice(REACH + nx, nx + 2 * REACH)
    rs_low, rs_mid, rs_high = slice(0, rim), slice(rim, rim + rows), slice(rim + rows, rows + 2 * rim)
    pl.when(ix == 0)(lambda: blank(xs_low, rs_mid))
    pl.when(ix == cx - 1)(lambda: blank(xs_high, rs_mid))
    pl.when(iy == 0)(lambda: blank(slice(None), rs_low))
    pl.when(iy == cy - 1)(lambda: blank(slice(None), rs_high))

    pl.semaphore_wait(barrier, n - 1 + ch - 1)
    swap(
        "gx", cx,
        send(kvg.at[REACH : 2 * REACH, rs_mid], kvg.at[xs_high, rs_mid], sem_h.at[0], sem_hr.at[0], {"gx": ix - 1}),
        send(kvg.at[nx : nx + REACH, rs_mid], kvg.at[xs_low, rs_mid], sem_h.at[1], sem_hr.at[1], {"gx": ix + 1}),
    )
    swap(
        "gy", cy,
        send(kvg.at[:, rim : 2 * rim], kvg.at[:, rs_high], sem_h.at[2], sem_hr.at[2], {"gy": iy - 1}),
        send(kvg.at[:, rows : rows + rim], kvg.at[:, rs_low], sem_h.at[3], sem_hr.at[3], {"gy": iy + 1}),
    )

    acc[...] = jnp.zeros_like(acc)
    wg[...] = jnp.zeros_like(wg)
    kx, kr = bx + 2 * REACH, (by + 2 * REACH) * depth
    qr = by * depth
    nq, nk = bx * qr, kx * kr
    across = ny // by

    def body(i, carry):
        x0 = (i // across) * bx
        r0 = pl.multiple_of(lax.rem(i, across) * qr, qr)
        mine = (pl.ds(x0, bx), pl.ds(r0, qr))
        wide = (pl.ds(x0, kx), pl.ds(r0, kr))
        tb = tok[mine].reshape(nq, -1)
        cb = cot[mine].reshape(nq, -1)
        q = (dot(tb, wq[...], 1, 0).astype(jnp.bfloat16).astype(jnp.float32) * scale).astype(jnp.bfloat16)
        u = dot(cb, wo[...], 1, 1).astype(jnp.bfloat16)
        keys = kvg[pl.ds(x0, kx), pl.ds(r0, kr), : 2 * HD].reshape(nk, 2 * HD)
        g1 = kvg[pl.ds(x0, kx), pl.ds(r0, kr), 2 * HD :].reshape(nk, 128).astype(jnp.float32)
        g1 = jnp.concatenate([g1] * (nq // 128), axis=1)
        s = jnp.where(table[...] > g1, dot(keys, q, 1, 1), -1e30)
        e = jnp.exp(s - jnp.max(s, axis=0, keepdims=True))
        p = (e * (1.0 / jnp.sum(e, axis=0, keepdims=True))).astype(jnp.bfloat16)
        o = dot(keys, p, 0, 0)
        r = jnp.sum(u.astype(jnp.float32).T * o, axis=0, keepdims=True)
        g = dot(keys, u, 1, 1)
        ds = (p.astype(jnp.float32) * (g - r)).astype(jnp.bfloat16)
        dq = dot(keys, ds, 0, 0) * scale
        dkv = dot(ds, q, 1, 0) + dot(p, u, 1, 0)
        acc[wide] += dkv.reshape(kx, kr, 2 * HD)
        wg[:HD] += dot(dq[:HD].astype(jnp.bfloat16), tb, 1, 0)
        wg[HD:] += dot(o[HD:].astype(jnp.bfloat16), cb, 1, 0)
        dq_all[mine] = dq.T.astype(jnp.bfloat16).reshape(bx, qr, 2 * HD)
        return carry

    lax.fori_loop(0, (nx // bx) * across, body, 0, unroll=2)

    sx[0] = acc[:REACH].astype(jnp.bfloat16)
    sx[1] = acc[REACH + nx :].astype(jnp.bfloat16)
    swap(
        "gx", cx,
        send(sx.at[0], rx.at[1], sem_h.at[4], sem_hr.at[4], {"gx": ix - 1}),
        send(sx.at[1], rx.at[0], sem_h.at[5], sem_hr.at[5], {"gx": ix + 1}),
    )
    cen[...] = acc[REACH : REACH + nx]

    @pl.when(ix > 0)
    def _():
        cen[:REACH] += rx[0].astype(jnp.float32)

    @pl.when(ix < cx - 1)
    def _():
        cen[nx - REACH :] += rx[1].astype(jnp.float32)

    sy[0] = cen[:, :rim].astype(jnp.bfloat16)
    sy[1] = cen[:, rim + rows :].astype(jnp.bfloat16)
    swap(
        "gy", cy,
        send(sy.at[0], ry.at[1], sem_h.at[6], sem_hr.at[6], {"gy": iy - 1}),
        send(sy.at[1], ry.at[0], sem_h.at[7], sem_hr.at[7], {"gy": iy + 1}),
    )

    @pl.when(iy > 0)
    def _():
        cen[:, rim : 2 * rim] += ry[0].astype(jnp.float32)

    @pl.when(iy < cy - 1)
    def _():
        cen[:, rows : rows + rim] += ry[1].astype(jnp.float32)

    dkv_all[...] = cen[:, rs_mid].astype(jnp.bfloat16)
    share = width // ch

    def product(j):
        cols = pl.ds(pl.multiple_of(j * share, 16), share)
        dkv = dkv_all[...].reshape(nx * rows, 2 * HD)
        dqs = dq_all[...].reshape(nx * rows, 2 * HD)
        return dot(wkv[cols, :], dkv, 1, 1) + dot(wq[cols, :], dqs, 1, 1)

    parts = []
    for k in range(1, ch):
        j = lax.rem(ih + k, ch)
        psend[k - 1] = product(j).astype(jnp.bfloat16)
        copy = send(psend.at[k - 1], precv.at[k - 1], sem_p.at[k - 1], sem_pr.at[k - 1], {"ha": j})
        copy.start()
        parts.append(copy)

    gsrc[: 2 * HD] = wg[...]
    gsrc[2 * HD :] = dot(
        dkv_all[...].reshape(nx * rows, 2 * HD), tok[...].reshape(nx * rows, width), 0, 0
    )
    piece = 4 * HD // n
    first = []
    for k in range(1, n):
        t, where = peer(k)
        src = gsrc.at[pl.ds(pl.multiple_of(t * piece, 8), piece)]
        copy = send(src, grecv.at[k - 1], sem_g.at[k - 1], sem_gr.at[k - 1], where)
        copy.start()
        first.append(copy)
    own[...] = product(ih)
    mine = pl.ds(pl.multiple_of(flat * piece, 8), piece)
    total = gsrc[mine]
    for k in range(1, n):
        first[k - 1].wait_recv()
        total += grecv[k - 1]
    gsum[mine] = total
    second = []
    for k in range(1, n):
        copy = send(gsum.at[mine], gsum.at[mine], sem_b.at[k - 1], sem_br.at[k - 1], peer(k)[1])
        copy.start()
        second.append(copy)
    for copy in first:
        copy.wait_send()
    for k in range(1, n):
        t = lax.rem(flat + n - k, n)
        other = gsum.at[pl.ds(pl.multiple_of(t * piece, 8), piece)]
        send(other, other, sem_b.at[k - 1], sem_br.at[k - 1], peer(k)[1]).wait_recv()
    for copy in second:
        copy.wait_send()
    norm = (n * nx * rows) ** (-0.5)
    everything = gsum[...] * norm
    output_out[...] = everything[HD : 2 * HD]
    input_out[:HD] = everything[:HD]
    input_out[HD:] = everything[2 * HD :]
    for copy in parts:
        copy.wait()
    summed = own[...]
    for k in range(1, ch):
        summed += precv[k - 1].astype(jnp.float32)
    token_out[...] = summed.T.astype(jnp.bfloat16)


def shards(tokens, input_weight, output_weight, tissue_bits, cotangent):
    nx, ny, depth, width = tokens.shape
    rows, rim = ny * depth, REACH * depth
    sizes = tuple(lax.axis_size(a) for a in ("gx", "gy", "ha"))
    n, ch = sizes[0] * sizes[1], sizes[2]
    tok = tokens.reshape(nx, rows, width)
    cot = cotangent.reshape(nx, rows, width)
    bx, by = tile_of(nx), tile_of(ny)
    table = jnp.asarray(mask_table(bx, by, depth))
    px, pr = nx + 2 * REACH, rows + 2 * rim
    bf, f32, dma = jnp.bfloat16, jnp.float32, pltpu.SemaphoreType.DMA
    share = width // ch
    token_gradient, input_gradient, output_gradient = pl.pallas_call(
        functools.partial(kernel, sizes, depth, bx, by),
        out_shape=(
            jax.ShapeDtypeStruct((nx * rows, share), bf),
            jax.ShapeDtypeStruct((3 * HD, width), f32),
            jax.ShapeDtypeStruct((HD, width), f32),
        ),
        in_specs=[VMEM] * 4 + [SMEM, VMEM],
        out_specs=(VMEM,) * 3,
        scratch_shapes=[
            pltpu.VMEM((width, 2 * HD), bf),
            pltpu.VMEM((width, 2 * HD), bf),
            pltpu.VMEM((2 * HD, width), bf),
            pltpu.VMEM((px, pr, 4 * HD), bf),
            pltpu.VMEM((px, pr, 2 * HD), f32),
            pltpu.VMEM((2 * HD, width), f32),
            pltpu.VMEM((nx, rows, 2 * HD), bf),
            pltpu.VMEM((nx, pr, 2 * HD), f32),
            pltpu.VMEM((nx, rows, 2 * HD), bf),
            pltpu.VMEM((2, REACH, pr, 2 * HD), bf),
            pltpu.VMEM((2, REACH, pr, 2 * HD), bf),
            pltpu.VMEM((2, nx, rim, 2 * HD), bf),
            pltpu.VMEM((2, nx, rim, 2 * HD), bf),
            pltpu.VMEM((ch - 1, share, nx * rows), bf),
            pltpu.VMEM((ch - 1, share, nx * rows), bf),
            pltpu.VMEM((share, nx * rows), f32),
            pltpu.VMEM((4 * HD, width), f32),
            pltpu.VMEM((n - 1, 4 * HD // n, width), f32),
            pltpu.VMEM((4 * HD, width), f32),
            dma((8,)), dma((8,)),
            dma((ch - 1,)), dma((ch - 1,)),
            dma((n - 1,)), dma((n - 1,)),
            dma((n - 1,)), dma((n - 1,)),
        ],
        compiler_params=pltpu.CompilerParams(
            collective_id=0, has_side_effects=True, vmem_limit_bytes=56 * 1024 * 1024
        ),
        name="whole",
    )(tok, cot, input_weight.T, output_weight, tissue_bits, table)
    return token_gradient.reshape(nx, ny, depth, share), input_gradient.T, output_gradient


def solution(mesh):
    placed = (
        P("gx", "gy", None, None),
        P(None, "ha"),
        P("ha", None),
        P("gx", "gy"),
        P("gx", "gy", None, None),
    )
    return jax.shard_map(
        shards,
        mesh=mesh,
        in_specs=placed,
        out_specs=(P("gx", "gy", None, "ha"), P(None, "ha"), P("ha", None)),
        check_vma=False,
    )
```

```python
import functools

import jax
import jax.numpy as jnp
import numpy as np
from jax import lax
from jax.experimental import pallas as pl
from jax.experimental.pallas import tpu as pltpu
from jax.sharding import PartitionSpec as P

HD = 64
REACH = 3
VMEM = pl.BlockSpec(memory_space=pltpu.VMEM)
SMEM = pl.BlockSpec(memory_space=pltpu.SMEM)
MESH = pl.DeviceIdType.MESH


def dot(a, b, ca, cb):
    return lax.dot_general(a, b, (((ca,), (cb,)), ((), ())), preferred_element_type=jnp.float32)


def tile_of(extent):
    return 4 if extent % 4 == 0 else extent


def mask_table(bx, by, depth):
    kx, ky = bx + 2 * REACH, by + 2 * REACH
    kg = np.stack(np.meshgrid(np.arange(kx) - REACH, np.arange(ky) - REACH, np.arange(depth), indexing="ij"), -1)
    qg = np.stack(np.meshgrid(np.arange(bx), np.arange(by), np.arange(depth), indexing="ij"), -1)
    far = np.abs(kg.reshape(-1, 1, 3) - qg.reshape(1, -1, 3)).max(-1)
    return ((far <= REACH).astype(np.float32) + (far == 0)).astype(np.float32)


def send(src, dst, send_sem, recv_sem, where):
    return pltpu.make_async_remote_copy(
        src_ref=src, dst_ref=dst, send_sem=send_sem, recv_sem=recv_sem, device_id=where, device_id_type=MESH
    )


def swap(axis, count, to_low, to_high):
    me = lax.axis_index(axis)
    has_low, has_high = me > 0, me < count - 1

    @pl.when(has_low)
    def _():
        to_low.start()

    @pl.when(has_high)
    def _():
        to_high.start()

    @pl.when(has_low)
    def _():
        to_low.wait_send()
        to_high.wait_recv()

    @pl.when(has_high)
    def _():
        to_high.wait_send()
        to_low.wait_recv()


def kernel(
    sizes, depth, bx, by, tok, cot, weights, outer, bits, table,
    token_out, input_out, output_out,
    wq, wkv, wo, kvg, acc, wg, dq_all, cen, dkv_all, sx, rx, sy, ry, psend, precv, own, gsrc, grecv, gsum,
    sem_h, sem_hr, sem_p, sem_pr, sem_g, sem_gr, sem_b, sem_br,
):
    cx, cy, ch = sizes
    nx, rows = tok.shape[0], tok.shape[1]
    ny, width = rows // depth, tok.shape[2]
    rim = REACH * depth
    scale = HD ** (-0.5)
    ix, iy, ih = lax.axis_index("gx"), lax.axis_index("gy"), lax.axis_index("ha")
    n = cx * cy
    flat = ix * cy + iy

    def peer(k):
        t = lax.rem(flat + k, n)
        return t, {"gx": t // cy, "gy": lax.rem(t, cy)}

    barrier = pltpu.get_barrier_semaphore()
    for k in range(1, n):
        pl.semaphore_signal(barrier, inc=1, device_id=peer(k)[1], device_id_type=MESH)
    for k in range(1, ch):
        pl.semaphore_signal(barrier, inc=1, device_id={"ha": lax.rem(ih + k, ch)}, device_id_type=MESH)

    turned = weights[...].astype(jnp.float32)
    blank_rows = jnp.zeros((HD, width), jnp.float32)
    wq[...] = jnp.concatenate([turned[:HD], blank_rows], axis=0).T.astype(jnp.bfloat16)
    wkv[...] = turned[HD:].T.astype(jnp.bfloat16)
    wo[:HD] = blank_rows.astype(jnp.bfloat16)
    wo[HD:] = outer[...]
    z = lax.broadcasted_iota(jnp.int32, (depth, 128), 0)

    def fill(x, carry):
        kvg[REACH + x, rim : rim + rows, : 2 * HD] = dot(tok[x], wkv[...], 1, 0).astype(jnp.bfloat16)
        for y in range(ny):
            live = jnp.right_shift(jnp.full((depth, 128), bits[x, y], jnp.int32), z) & 1
            kvg[REACH + x, rim + y * depth : rim + (y + 1) * depth, 2 * HD :] = (
                1.0 - live.astype(jnp.float32)
            ).astype(jnp.bfloat16)
        return carry

    lax.fori_loop(0, nx, fill, 0)

    def blank(where_x, where_r):
        shape = kvg.at[where_x, where_r, : 2 * HD].shape
        kvg[where_x, where_r, : 2 * HD] = jnp.zeros(shape, jnp.bfloat16)
        kvg[where_x, where_r, 2 * HD :] = jnp.ones(shape, jnp.bfloat16)

    xs_low, xs_high = slice(0, REACH), slice(REACH + nx, nx + 2 * REACH)
    rs_low, rs_mid, rs_high = slice(0, rim), slice(rim, rim + rows), slice(rim + rows, rows + 2 * rim)
    pl.when(ix == 0)(lambda: blank(xs_low, rs_mid))
    pl.when(ix == cx - 1)(lambda: blank(xs_high, rs_mid))
    pl.when(iy == 0)(lambda: blank(slice(None), rs_low))
    pl.when(iy == cy - 1)(lambda: blank(slice(None), rs_high))

    pl.semaphore_wait(barrier, n - 1 + ch - 1)
    swap(
        "gx", cx,
        send(kvg.at[REACH : 2 * REACH, rs_mid], kvg.at[xs_high, rs_mid], sem_h.at[0], sem_hr.at[0], {"gx": ix - 1}),
        send(kvg.at[nx : nx + REACH, rs_mid], kvg.at[xs_low, rs_mid], sem_h.at[1], sem_hr.at[1], {"gx": ix + 1}),
    )
    swap(
        "gy", cy,
        send(kvg.at[:, rim : 2 * rim], kvg.at[:, rs_high], sem_h.at[2], sem_hr.at[2], {"gy": iy - 1}),
        send(kvg.at[:, rows : rows + rim], kvg.at[:, rs_low], sem_h.at[3], sem_hr.at[3], {"gy": iy + 1}),
    )

    acc[...] = jnp.zeros_like(acc)
    wg[...] = jnp.zeros_like(wg)
    kx, kr = bx + 2 * REACH, (by + 2 * REACH) * depth
    qr = by * depth
    nq, nk = bx * qr, kx * kr
    across = ny // by

    def body(i, carry):
        x0 = (i // across) * bx
        r0 = pl.multiple_of(lax.rem(i, across) * qr, qr)
        mine = (pl.ds(x0, bx), pl.ds(r0, qr))
        wide = (pl.ds(x0, kx), pl.ds(r0, kr))
        tb = tok[mine].reshape(nq, -1)
        cb = cot[mine].reshape(nq, -1)
        q = (dot(tb, wq[...], 1, 0).astype(jnp.bfloat16).astype(jnp.float32) * scale).astype(jnp.bfloat16)
        u = dot(cb, wo[...], 1, 1).astype(jnp.bfloat16)
        keys = kvg[pl.ds(x0, kx), pl.ds(r0, kr), : 2 * HD].reshape(nk, 2 * HD)
        g1 = kvg[pl.ds(x0, kx), pl.ds(r0, kr), 2 * HD :].reshape(nk, 128).astype(jnp.float32)
        g1 = jnp.concatenate([g1] * (nq // 128), axis=1)
        s = jnp.where(table[...] > g1, dot(keys, q, 1, 1), -1e30)
        e = jnp.exp(s - jnp.max(s, axis=0, keepdims=True))
        p = (e * (1.0 / jnp.sum(e, axis=0, keepdims=True))).astype(jnp.bfloat16)
        o = dot(keys, p, 0, 0)
        r = jnp.sum(u.astype(jnp.float32).T * o, axis=0, keepdims=True)
        g = dot(keys, u, 1, 1)
        ds = (p.astype(jnp.float32) * (g - r)).astype(jnp.bfloat16)
        dq = dot(keys, ds, 0, 0) * scale
        dkv = dot(ds, q, 1, 0) + dot(p, u, 1, 0)
        acc[wide] += dkv.reshape(kx, kr, 2 * HD)
        wg[:HD] += dot(dq[:HD].astype(jnp.bfloat16), tb, 1, 0)
        wg[HD:] += dot(o[HD:].astype(jnp.bfloat16), cb, 1, 0)
        dq_all[mine] = dq.T.astype(jnp.bfloat16).reshape(bx, qr, 2 * HD)
        return carry

    lax.fori_loop(0, (nx // bx) * across, body, 0, unroll=2)

    sx[0] = acc[:REACH].astype(jnp.bfloat16)
    sx[1] = acc[REACH + nx :].astype(jnp.bfloat16)
    swap(
        "gx", cx,
        send(sx.at[0], rx.at[1], sem_h.at[4], sem_hr.at[4], {"gx": ix - 1}),
        send(sx.at[1], rx.at[0], sem_h.at[5], sem_hr.at[5], {"gx": ix + 1}),
    )
    cen[...] = acc[REACH : REACH + nx]

    @pl.when(ix > 0)
    def _():
        cen[:REACH] += rx[0].astype(jnp.float32)

    @pl.when(ix < cx - 1)
    def _():
        cen[nx - REACH :] += rx[1].astype(jnp.float32)

    sy[0] = cen[:, :rim].astype(jnp.bfloat16)
    sy[1] = cen[:, rim + rows :].astype(jnp.bfloat16)
    swap(
        "gy", cy,
        send(sy.at[0], ry.at[1], sem_h.at[6], sem_hr.at[6], {"gy": iy - 1}),
        send(sy.at[1], ry.at[0], sem_h.at[7], sem_hr.at[7], {"gy": iy + 1}),
    )

    @pl.when(iy > 0)
    def _():
        cen[:, rim : 2 * rim] += ry[0].astype(jnp.float32)

    @pl.when(iy < cy - 1)
    def _():
        cen[:, rows : rows + rim] += ry[1].astype(jnp.float32)

    dkv_all[...] = cen[:, rs_mid].astype(jnp.bfloat16)
    share = width // ch

    half = nx // 2
    halves = (0, 1)
    near = ih + 1 - 2 * lax.rem(ih, 2)
    far, corner = lax.rem(ih + 2, ch), lax.rem(near + 2, ch)

    def product(j, h):
        cols = pl.ds(pl.multiple_of(j * share, 16), share)
        dkv = dkv_all[h * half : (h + 1) * half].reshape(half * rows, 2 * HD)
        dqs = dq_all[h * half : (h + 1) * half].reshape(half * rows, 2 * HD)
        return dot(wkv[cols, :], dkv, 1, 1) + dot(wq[cols, :], dqs, 1, 1)

    def hop(slot, h, where):
        i = 2 * slot + h
        return send(psend.at[i], precv.at[i], sem_p.at[i], sem_pr.at[i], {"ha": where})

    relay = [hop(0, h, near) for h in halves]
    close = [hop(1, h, near) for h in halves]
    long = [hop(2, h, far) for h in halves]
    for h in halves:
        psend[h] = product(corner, h).astype(jnp.bfloat16)
        relay[h].start()

    gsrc[: 2 * HD] = wg[...]
    gsrc[2 * HD :] = dot(
        dkv_all[...].reshape(nx * rows, 2 * HD), tok[...].reshape(nx * rows, width), 0, 0
    )
    piece = 4 * HD // n
    first = []
    for k in range(1, n):
        t, where = peer(k)
        src = gsrc.at[pl.ds(pl.multiple_of(t * piece, 8), piece)]
        copy = send(src, grecv.at[k - 1], sem_g.at[k - 1], sem_gr.at[k - 1], where)
        copy.start()
        first.append(copy)
    for h in halves:
        psend[2 + h] = product(near, h).astype(jnp.bfloat16)
    for h in halves:
        mixed = product(far, h)
        relay[h].wait_recv()
        psend[4 + h] = (mixed + precv[h].astype(jnp.float32)).astype(jnp.bfloat16)
        long[h].start()
    for h in halves:
        close[h].start()
        own[h] = product(ih, h)
    mine = pl.ds(pl.multiple_of(flat * piece, 8), piece)
    total = gsrc[mine]
    for k in range(1, n):
        first[k - 1].wait_recv()
        total += grecv[k - 1]
    gsum[mine] = total
    second = []
    for k in range(1, n):
        copy = send(gsum.at[mine], gsum.at[mine], sem_b.at[k - 1], sem_br.at[k - 1], peer(k)[1])
        copy.start()
        second.append(copy)
    for copy in first:
        copy.wait_send()
    for k in range(1, n):
        t = lax.rem(flat + n - k, n)
        other = gsum.at[pl.ds(pl.multiple_of(t * piece, 8), piece)]
        send(other, other, sem_b.at[k - 1], sem_br.at[k - 1], peer(k)[1]).wait_recv()
    for copy in second:
        copy.wait_send()
    norm = (n * nx * rows) ** (-0.5)
    everything = gsum[...] * norm
    output_out[...] = everything[HD : 2 * HD]
    input_out[:HD] = everything[:HD]
    input_out[HD:] = everything[2 * HD :]
    for h in halves:
        long[h].wait_recv()
        close[h].wait_recv()
        summed = own[h] + precv[2 + h].astype(jnp.float32) + precv[4 + h].astype(jnp.float32)
        token_out[h * half * rows : (h + 1) * half * rows] = summed.T.astype(jnp.bfloat16)
    for copy in relay + close + long:
        copy.wait_send()


def shards(tokens, input_weight, output_weight, tissue_bits, cotangent):
    nx, ny, depth, width = tokens.shape
    rows, rim = ny * depth, REACH * depth
    sizes = tuple(lax.axis_size(a) for a in ("gx", "gy", "ha"))
    n, ch = sizes[0] * sizes[1], sizes[2]
    tok = tokens.reshape(nx, rows, width)
    cot = cotangent.reshape(nx, rows, width)
    bx, by = tile_of(nx), tile_of(ny)
    table = jnp.asarray(mask_table(bx, by, depth))
    px, pr = nx + 2 * REACH, rows + 2 * rim
    bf, f32, dma = jnp.bfloat16, jnp.float32, pltpu.SemaphoreType.DMA
    share = width // ch
    token_gradient, input_gradient, output_gradient = pl.pallas_call(
        functools.partial(kernel, sizes, depth, bx, by),
        out_shape=(
            jax.ShapeDtypeStruct((nx * rows, share), bf),
            jax.ShapeDtypeStruct((3 * HD, width), f32),
            jax.ShapeDtypeStruct((HD, width), f32),
        ),
        in_specs=[VMEM] * 4 + [SMEM, VMEM],
        out_specs=(VMEM,) * 3,
        scratch_shapes=[
            pltpu.VMEM((width, 2 * HD), bf),
            pltpu.VMEM((width, 2 * HD), bf),
            pltpu.VMEM((2 * HD, width), bf),
            pltpu.VMEM((px, pr, 4 * HD), bf),
            pltpu.VMEM((px, pr, 2 * HD), f32),
            pltpu.VMEM((2 * HD, width), f32),
            pltpu.VMEM((nx, rows, 2 * HD), bf),
            pltpu.VMEM((nx, pr, 2 * HD), f32),
            pltpu.VMEM((nx, rows, 2 * HD), bf),
            pltpu.VMEM((2, REACH, pr, 2 * HD), bf),
            pltpu.VMEM((2, REACH, pr, 2 * HD), bf),
            pltpu.VMEM((2, nx, rim, 2 * HD), bf),
            pltpu.VMEM((2, nx, rim, 2 * HD), bf),
            pltpu.VMEM((6, share, nx * rows // 2), bf),
            pltpu.VMEM((6, share, nx * rows // 2), bf),
            pltpu.VMEM((2, share, nx * rows // 2), f32),
            pltpu.VMEM((4 * HD, width), f32),
            pltpu.VMEM((n - 1, 4 * HD // n, width), f32),
            pltpu.VMEM((4 * HD, width), f32),
            dma((8,)), dma((8,)),
            dma((6,)), dma((6,)),
            dma((n - 1,)), dma((n - 1,)),
            dma((n - 1,)), dma((n - 1,)),
        ],
        compiler_params=pltpu.CompilerParams(
            collective_id=0, has_side_effects=True, vmem_limit_bytes=56 * 1024 * 1024
        ),
        name="whole",
    )(tok, cot, input_weight.T, output_weight, tissue_bits, table)
    return token_gradient.reshape(nx, ny, depth, share), input_gradient.T, output_gradient


def solution(mesh):
    placed = (
        P("gx", "gy", None, None),
        P(None, "ha"),
        P("ha", None),
        P("gx", "gy"),
        P("gx", "gy", None, None),
    )
    return jax.shard_map(
        shards,
        mesh=mesh,
        in_specs=placed,
        out_specs=(P("gx", "gy", None, "ha"), P(None, "ha"), P("ha", None)),
        check_vma=False,
    )
```

```python
import functools

import jax
import jax.numpy as jnp
import numpy as np
from jax import lax
from jax.experimental import pallas as pl
from jax.experimental.pallas import tpu as pltpu
from jax.sharding import PartitionSpec as P

HD = 64
REACH = 3
VMEM = pl.BlockSpec(memory_space=pltpu.VMEM)
SMEM = pl.BlockSpec(memory_space=pltpu.SMEM)
MESH = pl.DeviceIdType.MESH


def dot(a, b, ca, cb):
    return lax.dot_general(a, b, (((ca,), (cb,)), ((), ())), preferred_element_type=jnp.float32)


def tile_of(extent):
    return 4 if extent % 4 == 0 else extent


def mask_table(bx, by, depth):
    kx, ky = bx + 2 * REACH, by + 2 * REACH
    kg = np.stack(np.meshgrid(np.arange(kx) - REACH, np.arange(ky) - REACH, np.arange(depth), indexing="ij"), -1)
    qg = np.stack(np.meshgrid(np.arange(bx), np.arange(by), np.arange(depth), indexing="ij"), -1)
    far = np.abs(kg.reshape(-1, 1, 3) - qg.reshape(1, -1, 3)).max(-1)
    return ((far <= REACH).astype(np.float32) + (far == 0)).astype(np.float32)


def send(src, dst, send_sem, recv_sem, where):
    return pltpu.make_async_remote_copy(
        src_ref=src, dst_ref=dst, send_sem=send_sem, recv_sem=recv_sem, device_id=where, device_id_type=MESH
    )


def swap(axis, count, to_low, to_high):
    me = lax.axis_index(axis)
    has_low, has_high = me > 0, me < count - 1

    @pl.when(has_low)
    def _():
        to_low.start()

    @pl.when(has_high)
    def _():
        to_high.start()

    @pl.when(has_low)
    def _():
        to_low.wait_send()
        to_high.wait_recv()

    @pl.when(has_high)
    def _():
        to_high.wait_send()
        to_low.wait_recv()


def kernel(
    sizes, depth, bx, by, tok, cot, weights, outer, bits, table,
    token_out, input_out, output_out,
    wq, wkv, wo, kvg, acc, wg, dq_all, cen, dkv_all, sx, rx, sy, ry, psend, precv, own, gsrc, grecv, gsum,
    sem_h, sem_hr, sem_p, sem_pr, sem_g, sem_gr, sem_b, sem_br,
):
    cx, cy, ch = sizes
    nx, rows = tok.shape[0], tok.shape[1]
    ny, width = rows // depth, tok.shape[2]
    rim = REACH * depth
    scale = HD ** (-0.5)
    ix, iy, ih = lax.axis_index("gx"), lax.axis_index("gy"), lax.axis_index("ha")
    n = cx * cy
    flat = ix * cy + iy

    def peer(k):
        t = lax.rem(flat + k, n)
        return t, {"gx": t // cy, "gy": lax.rem(t, cy)}

    barrier = pltpu.get_barrier_semaphore()
    for k in range(1, n):
        pl.semaphore_signal(barrier, inc=1, device_id=peer(k)[1], device_id_type=MESH)
    for k in range(1, ch):
        pl.semaphore_signal(barrier, inc=1, device_id={"ha": lax.rem(ih + k, ch)}, device_id_type=MESH)

    turned = weights[...].astype(jnp.float32)
    blank_rows = jnp.zeros((HD, width), jnp.float32)
    wq[...] = jnp.concatenate([turned[:HD], blank_rows], axis=0).T.astype(jnp.bfloat16)
    wkv[...] = turned[HD:].T.astype(jnp.bfloat16)
    wo[:HD] = blank_rows.astype(jnp.bfloat16)
    wo[HD:] = outer[...]
    z = lax.broadcasted_iota(jnp.int32, (depth, 128), 0)

    def fill(x, carry):
        kvg[REACH + x, rim : rim + rows, : 2 * HD] = dot(tok[x], wkv[...], 1, 0).astype(jnp.bfloat16)
        for y in range(ny):
            live = jnp.right_shift(jnp.full((depth, 128), bits[x, y], jnp.int32), z) & 1
            kvg[REACH + x, rim + y * depth : rim + (y + 1) * depth, 2 * HD :] = (
                1.0 - live.astype(jnp.float32)
            ).astype(jnp.bfloat16)
        return carry

    lax.fori_loop(0, nx, fill, 0)

    def blank(where_x, where_r):
        shape = kvg.at[where_x, where_r, : 2 * HD].shape
        kvg[where_x, where_r, : 2 * HD] = jnp.zeros(shape, jnp.bfloat16)
        kvg[where_x, where_r, 2 * HD :] = jnp.ones(shape, jnp.bfloat16)

    xs_low, xs_high = slice(0, REACH), slice(REACH + nx, nx + 2 * REACH)
    rs_low, rs_mid, rs_high = slice(0, rim), slice(rim, rim + rows), slice(rim + rows, rows + 2 * rim)
    pl.when(ix == 0)(lambda: blank(xs_low, rs_mid))
    pl.when(ix == cx - 1)(lambda: blank(xs_high, rs_mid))
    pl.when(iy == 0)(lambda: blank(slice(None), rs_low))
    pl.when(iy == cy - 1)(lambda: blank(slice(None), rs_high))

    pl.semaphore_wait(barrier, n - 1 + ch - 1)
    swap(
        "gx", cx,
        send(kvg.at[REACH : 2 * REACH, rs_mid], kvg.at[xs_high, rs_mid], sem_h.at[0], sem_hr.at[0], {"gx": ix - 1}),
        send(kvg.at[nx : nx + REACH, rs_mid], kvg.at[xs_low, rs_mid], sem_h.at[1], sem_hr.at[1], {"gx": ix + 1}),
    )
    swap(
        "gy", cy,
        send(kvg.at[:, rim : 2 * rim], kvg.at[:, rs_high], sem_h.at[2], sem_hr.at[2], {"gy": iy - 1}),
        send(kvg.at[:, rows : rows + rim], kvg.at[:, rs_low], sem_h.at[3], sem_hr.at[3], {"gy": iy + 1}),
    )

    acc[...] = jnp.zeros_like(acc)
    wg[...] = jnp.zeros_like(wg)
    kx, kr = bx + 2 * REACH, (by + 2 * REACH) * depth
    qr = by * depth
    nq, nk = bx * qr, kx * kr
    across = ny // by

    def body(i, carry):
        x0 = (i // across) * bx
        r0 = pl.multiple_of(lax.rem(i, across) * qr, qr)
        mine = (pl.ds(x0, bx), pl.ds(r0, qr))
        wide = (pl.ds(x0, kx), pl.ds(r0, kr))
        tb = tok[mine].reshape(nq, -1)
        cb = cot[mine].reshape(nq, -1)
        q = (dot(tb, wq[...], 1, 0).astype(jnp.bfloat16).astype(jnp.float32) * scale).astype(jnp.bfloat16)
        u = dot(cb, wo[...], 1, 1).astype(jnp.bfloat16)
        keys = kvg[pl.ds(x0, kx), pl.ds(r0, kr), : 2 * HD].reshape(nk, 2 * HD)
        g1 = kvg[pl.ds(x0, kx), pl.ds(r0, kr), 2 * HD :].reshape(nk, 128).astype(jnp.float32)
        g1 = jnp.concatenate([g1] * (nq // 128), axis=1)
        s = jnp.where(table[...] > g1, dot(keys, q, 1, 1), -1e30)
        e = jnp.exp(s - jnp.max(s, axis=0, keepdims=True))
        p = (e * (1.0 / jnp.sum(e, axis=0, keepdims=True))).astype(jnp.bfloat16)
        o = dot(keys, p, 0, 0)
        r = jnp.sum(u.astype(jnp.float32).T * o, axis=0, keepdims=True)
        g = dot(keys, u, 1, 1)
        ds = (p.astype(jnp.float32) * (g - r)).astype(jnp.bfloat16)
        dq = dot(keys, ds, 0, 0) * scale
        dkv = dot(ds, q, 1, 0) + dot(p, u, 1, 0)
        acc[wide] += dkv.reshape(kx, kr, 2 * HD)
        wg[:HD] += dot(dq[:HD].astype(jnp.bfloat16), tb, 1, 0)
        wg[HD:] += dot(o[HD:].astype(jnp.bfloat16), cb, 1, 0)
        dq_all[mine] = dq.T.astype(jnp.bfloat16).reshape(bx, qr, 2 * HD)
        return carry

    lax.fori_loop(0, (nx // bx) * across, body, 0, unroll=2)

    sx[0] = acc[:REACH].astype(jnp.bfloat16)
    sx[1] = acc[REACH + nx :].astype(jnp.bfloat16)
    swap(
        "gx", cx,
        send(sx.at[0], rx.at[1], sem_h.at[4], sem_hr.at[4], {"gx": ix - 1}),
        send(sx.at[1], rx.at[0], sem_h.at[5], sem_hr.at[5], {"gx": ix + 1}),
    )
    cen[...] = acc[REACH : REACH + nx]

    @pl.when(ix > 0)
    def _():
        cen[:REACH] += rx[0].astype(jnp.float32)

    @pl.when(ix < cx - 1)
    def _():
        cen[nx - REACH :] += rx[1].astype(jnp.float32)

    sy[0] = cen[:, :rim].astype(jnp.bfloat16)
    sy[1] = cen[:, rim + rows :].astype(jnp.bfloat16)
    swap(
        "gy", cy,
        send(sy.at[0], ry.at[1], sem_h.at[6], sem_hr.at[6], {"gy": iy - 1}),
        send(sy.at[1], ry.at[0], sem_h.at[7], sem_hr.at[7], {"gy": iy + 1}),
    )

    @pl.when(iy > 0)
    def _():
        cen[:, rim : 2 * rim] += ry[0].astype(jnp.float32)

    @pl.when(iy < cy - 1)
    def _():
        cen[:, rows : rows + rim] += ry[1].astype(jnp.float32)

    dkv_all[...] = cen[:, rs_mid].astype(jnp.bfloat16)
    share = width // ch

    pieces = psend.shape[0] // 3
    half = nx // pieces
    halves = range(pieces)
    near = ih + 1 - 2 * lax.rem(ih, 2)
    far, corner = lax.rem(ih + 2, ch), lax.rem(near + 2, ch)

    def product(j, h):
        cols = pl.ds(pl.multiple_of(j * share, 16), share)
        dkv = dkv_all[h * half : (h + 1) * half].reshape(half * rows, 2 * HD)
        dqs = dq_all[h * half : (h + 1) * half].reshape(half * rows, 2 * HD)
        return dot(wkv[cols, :], dkv, 1, 1) + dot(wq[cols, :], dqs, 1, 1)

    def hop(slot, h, where):
        i = pieces * slot + h
        return send(psend.at[i], precv.at[i], sem_p.at[i], sem_pr.at[i], {"ha": where})

    relay = [hop(0, h, near) for h in halves]
    close = [hop(1, h, near) for h in halves]
    long = [hop(2, h, far) for h in halves]
    for h in halves:
        psend[h] = product(corner, h).astype(jnp.bfloat16)
        relay[h].start()

    gsrc[: 2 * HD] = wg[...]
    gsrc[2 * HD :] = dot(
        dkv_all[...].reshape(nx * rows, 2 * HD), tok[...].reshape(nx * rows, width), 0, 0
    )
    piece = 4 * HD // n
    first = []
    for k in range(1, n):
        t, where = peer(k)
        src = gsrc.at[pl.ds(pl.multiple_of(t * piece, 8), piece)]
        copy = send(src, grecv.at[k - 1], sem_g.at[k - 1], sem_gr.at[k - 1], where)
        copy.start()
        first.append(copy)
    for h in halves:
        psend[pieces + h] = product(near, h).astype(jnp.bfloat16)
    for h in halves:
        mixed = product(far, h)
        relay[h].wait_recv()
        psend[2 * pieces + h] = (mixed + precv[h].astype(jnp.float32)).astype(jnp.bfloat16)
        long[h].start()
    for h in halves:
        close[h].start()
        own[h] = product(ih, h)
    mine = pl.ds(pl.multiple_of(flat * piece, 8), piece)
    total = gsrc[mine]
    for k in range(1, n):
        first[k - 1].wait_recv()
        total += grecv[k - 1]
    gsum[mine] = total
    second = []
    for k in range(1, n):
        copy = send(gsum.at[mine], gsum.at[mine], sem_b.at[k - 1], sem_br.at[k - 1], peer(k)[1])
        copy.start()
        second.append(copy)
    for copy in first:
        copy.wait_send()
    for k in range(1, n):
        t = lax.rem(flat + n - k, n)
        other = gsum.at[pl.ds(pl.multiple_of(t * piece, 8), piece)]
        send(other, other, sem_b.at[k - 1], sem_br.at[k - 1], peer(k)[1]).wait_recv()
    for copy in second:
        copy.wait_send()
    norm = (n * nx * rows) ** (-0.5)
    everything = gsum[...] * norm
    output_out[...] = everything[HD : 2 * HD]
    input_out[:HD] = everything[:HD]
    input_out[HD:] = everything[2 * HD :]
    for h in halves:
        long[h].wait_recv()
        close[h].wait_recv()
        summed = own[h] + precv[pieces + h].astype(jnp.float32) + precv[2 * pieces + h].astype(jnp.float32)
        token_out[h * half * rows : (h + 1) * half * rows] = summed.T.astype(jnp.bfloat16)
    for copy in relay + close + long:
        copy.wait_send()


def shards(tokens, input_weight, output_weight, tissue_bits, cotangent):
    nx, ny, depth, width = tokens.shape
    rows, rim = ny * depth, REACH * depth
    sizes = tuple(lax.axis_size(a) for a in ("gx", "gy", "ha"))
    n, ch = sizes[0] * sizes[1], sizes[2]
    tok = tokens.reshape(nx, rows, width)
    cot = cotangent.reshape(nx, rows, width)
    bx, by = tile_of(nx), tile_of(ny)
    table = jnp.asarray(mask_table(bx, by, depth))
    px, pr = nx + 2 * REACH, rows + 2 * rim
    bf, f32, dma = jnp.bfloat16, jnp.float32, pltpu.SemaphoreType.DMA
    share = width // ch
    pieces = 4 if nx % 4 == 0 else 1
    token_gradient, input_gradient, output_gradient = pl.pallas_call(
        functools.partial(kernel, sizes, depth, bx, by),
        out_shape=(
            jax.ShapeDtypeStruct((nx * rows, share), bf),
            jax.ShapeDtypeStruct((3 * HD, width), f32),
            jax.ShapeDtypeStruct((HD, width), f32),
        ),
        in_specs=[VMEM] * 4 + [SMEM, VMEM],
        out_specs=(VMEM,) * 3,
        scratch_shapes=[
            pltpu.VMEM((width, 2 * HD), bf),
            pltpu.VMEM((width, 2 * HD), bf),
            pltpu.VMEM((2 * HD, width), bf),
            pltpu.VMEM((px, pr, 4 * HD), bf),
            pltpu.VMEM((px, pr, 2 * HD), f32),
            pltpu.VMEM((2 * HD, width), f32),
            pltpu.VMEM((nx, rows, 2 * HD), bf),
            pltpu.VMEM((nx, pr, 2 * HD), f32),
            pltpu.VMEM((nx, rows, 2 * HD), bf),
            pltpu.VMEM((2, REACH, pr, 2 * HD), bf),
            pltpu.VMEM((2, REACH, pr, 2 * HD), bf),
            pltpu.VMEM((2, nx, rim, 2 * HD), bf),
            pltpu.VMEM((2, nx, rim, 2 * HD), bf),
            pltpu.VMEM((3 * pieces, share, nx * rows // pieces), bf),
            pltpu.VMEM((3 * pieces, share, nx * rows // pieces), bf),
            pltpu.VMEM((pieces, share, nx * rows // pieces), f32),
            pltpu.VMEM((4 * HD, width), f32),
            pltpu.VMEM((n - 1, 4 * HD // n, width), f32),
            pltpu.VMEM((4 * HD, width), f32),
            dma((8,)), dma((8,)),
            dma((3 * pieces,)), dma((3 * pieces,)),
            dma((n - 1,)), dma((n - 1,)),
            dma((n - 1,)), dma((n - 1,)),
        ],
        compiler_params=pltpu.CompilerParams(
            collective_id=0, has_side_effects=True, vmem_limit_bytes=56 * 1024 * 1024
        ),
        name="whole",
    )(tok, cot, input_weight.T, output_weight, tissue_bits, table)
    return token_gradient.reshape(nx, ny, depth, share), input_gradient.T, output_gradient


def solution(mesh):
    placed = (
        P("gx", "gy", None, None),
        P(None, "ha"),
        P("ha", None),
        P("gx", "gy"),
        P("gx", "gy", None, None),
    )
    return jax.shard_map(
        shards,
        mesh=mesh,
        in_specs=placed,
        out_specs=(P("gx", "gy", None, "ha"), P(None, "ha"), P("ha", None)),
        check_vma=False,
    )
```
